256 devices in a mesh: section: 16 (over x, z_hi), tensor: 16 (over z_lo, y, core).
Axes of the slice: x: 4, y: 4, z: 8 (z_hi: 4, z_lo: 2; z = z_hi * 2 + z_lo), core: 2. Of those that a mesh axis runs over, the one named last changes fastest.
Arguments:
- inputs: bfloat16 [8192, 4096], P('section'), may hold values from -6 to 6
- out_grads: bfloat16 [8192, 11008], P('section', 'tensor'), may hold values from -0.1796875 to 0.1796875
- use_section: int32 [6], replicated, may hold values from 0 to 15, as said below
- a_inverse: float32 [4096, 256], P('section'), may hold values from -0.375 to 0.375
- g_inverse: float32 [11008, 688], P('tensor'), may hold values from -0.21875 to 0.21875
Outputs:
- a_cov: float32 [4096, 4096], P('section', 'tensor')
- g_cov: float32 [11008, 11008], P('section', 'tensor')
- grad: float32 [4096, 11008], P('section', 'tensor')
- precond: float32 [4096, 11008], P('section', 'tensor')
The draws below stay inside these ranges and needn't reach their ends.
Inputs may be any that keep to these rules, and one draw needn't show every extreme that they name: `use_section`: the entries are distinct copies; the first and the last copy are always among them.
All inputs are finite; a program needn't handle non-finite values.
Results may differ from the reference program's by a relative error of at most 0.015.
Values may be sent and summed in bfloat16 or wider, within the bound.
A program may use at most 128 MiB of HBM per device.

```python
import jax
import jax.numpy as jnp
from jax import lax

D = 4096
FF = 11008
TOK_DEV = 512
USES = 6
TOKENS = 8192
DB = 256
FB = 688
N_SECTION = 16
N_TENSOR = 16


def draw_use_section(key, part):
    key = jax.random.fold_in(key, 7)
    inner_key, order_key = jax.random.split(key)
    middle = 1 + jax.random.permutation(inner_key, N_SECTION - 2)[:USES - 2]
    ends = jnp.array([0, N_SECTION - 1], jnp.int32)
    chosen = jnp.concatenate([ends, middle.astype(jnp.int32)])
    order = jax.random.permutation(order_key, USES)
    return chosen[order].astype(jnp.int32)


def shard_levels(key, dims, pieces, smallest, high):
    level = 1.0
    for position, blocks in pieces:
        steps = jax.random.uniform(jax.random.fold_in(jax.random.fold_in(key, 6), position), (blocks,), jnp.float32, smallest / len(pieces), high / len(pieces))
        level = level * jnp.repeat(jnp.exp(steps), dims[position] // blocks).reshape((-1,) + (1,) * (len(dims) - 1 - position))
    return level


def normal_values(stream_key, dims, scale, reach, cuts=(), held_as=jnp.bfloat16):
    entries = scale * jax.random.normal(stream_key, dims, jnp.float32)
    if cuts:
        entries = entries * shard_levels(stream_key, dims, cuts, -0.22, 0.18)
    return jnp.clip(entries, -reach, reach).astype(held_as)


def setup_inputs(seed: int = 0) -> dict:
    key_of = jax.random.split(jax.random.key(seed), 6)
    return {
        "inputs": normal_values(key_of[0], (TOKENS, D), 1.0, 6.0, ((0, 16),)),
        "out_grads": normal_values(key_of[1], (TOKENS, FF), 0.03, 0.1796875, ((0, 16), (1, 16))),
        "use_section": draw_use_section(jax.random.fold_in(key_of[5], 71), 0),
        "a_inverse": normal_values(key_of[3], (D, DB), DB ** -0.5, 0.375, ((0, 16),), jnp.float32),
        "g_inverse": normal_values(key_of[4], (FF, FB), FB ** -0.5, 0.21875, ((0, 16),), jnp.float32),
    }


def cross(left, right):
    return lax.dot_general(left, right, (((0,), (0,)), ((), ())), preferred_element_type=jnp.float32)


def rounded(value):
    return lax.optimization_barrier(value.astype(jnp.bfloat16)).astype(jnp.float32)


def reference(inputs, out_grads, use_section, a_inverse, g_inverse):
    a_sum = jnp.zeros((D, D), jnp.float32)
    g_sum = jnp.zeros((FF, FF), jnp.float32)
    w_sum = jnp.zeros((D, FF), jnp.float32)
    for usage in range(USES):
        start = (use_section[usage] * TOK_DEV).astype(jnp.int32)
        rows_a = lax.dynamic_slice_in_dim(inputs, start, TOK_DEV, 0)
        rows_g = lax.dynamic_slice_in_dim(out_grads, start, TOK_DEV, 0)
        a_sum = a_sum + rounded(cross(rows_a, rows_a))
        g_sum = g_sum + rounded(cross(rows_g, rows_g))
        w_sum = w_sum + rounded(cross(rows_a, rows_g))
    a_cov = a_sum / (USES * TOK_DEV)
    blocks_a = a_inverse.reshape(N_SECTION, DB, DB)
    blocks_g = g_inverse.reshape(N_TENSOR, FB, FB)
    grad_four = w_sum.reshape(N_SECTION, DB, N_TENSOR, FB)
    left = jnp.einsum("sij,sjtk->sitk", blocks_a, grad_four, precision=lax.Precision.HIGHEST)
    both = jnp.einsum("sitk,tkl->sitl", left, blocks_g, precision=lax.Precision.HIGHEST)
    return a_cov, g_sum, w_sum, both.reshape(D, FF)
```

```python
import jax
import jax.numpy as jnp
from jax import lax
from jax.experimental import pallas as pl
from jax.experimental.pallas import tpu as pltpu
from jax.sharding import PartitionSpec as P

TOK_DEV = 512
USES = 6
N = 16
D = 4096
DB = 256
FB = 688
SUB = 16
PIECE = USES * SUB
HALF = N * PIECE
GA, X, GB = 0, 1, 2
MESH = pl.DeviceIdType.MESH


def cross(left, right):
    return lax.dot_general(
        left, right, (((0,), (0,)), ((), ())), preferred_element_type=jnp.float32
    )


def aligned(value, step):
    return pl.multiple_of(value * step, step)


def kernel(
    inp, grads, use, a_inv, g_inv, a_out, g_out, w_out, p_out,
    rg0, rg1, rx, fg, fx, sg, sx, acc_a, acc_g, acc_w, acc_p, ai, gi, ss, rs, ls,
):
    s, t = lax.axis_index("section"), lax.axis_index("tensor")
    x, z = s // 4, s % 4
    l, y, c = t // 8, (t // 2) % 4, t % 2

    def sec(dx, dz):
        return ((x + dx + 4) % 4) * 4 + (z + dz + 4) % 4

    def ten(dl, dy, dc):
        return (((l + dl) % 2) * 4 + (y + dy + 4) % 4) * 2 + (c + dc) % 2

    bar = pltpu.get_barrier_semaphore()
    for k in range(1, N):
        pl.semaphore_signal(bar, inc=1, device_id=((s + k) % N, t), device_id_type=MESH)
    for d in (ten(1, 0, 0), ten(0, 1, 0), ten(0, -1, 0), ten(0, 0, 1)):
        pl.semaphore_signal(bar, inc=1, device_id=(s, d), device_id_type=MESH)

    @pl.when(s != t)
    def _():
        pl.semaphore_signal(bar, inc=1, device_id=(t, s), device_id_type=MESH)

    loads = [
        pltpu.make_async_copy(a_inv, ai, ls.at[0]),
        pltpu.make_async_copy(g_inv, gi, ls.at[1]),
    ]

    def share(ch, p):
        if ch == X:
            return inp.at[pl.ds(aligned(p, 2 * SUB), 2 * SUB), pl.ds(aligned(t, DB), DB)]
        h = ch // 2
        return grads.at[pl.ds(pl.multiple_of(p * 2 * SUB + h * SUB, SUB), SUB)]

    def slot(ch, k):
        return (rg0, rx, rg1)[ch].at[k]

    own = [pltpu.make_async_copy(share(ch, s), slot(ch, N - 1), ls.at[2 + ch]) for ch in range(3)]
    for cp in loads + own:
        cp.start()
    pl.semaphore_wait(bar, 19 + (s != t).astype(jnp.int32))

    ids = {}

    def sem(key):
        return ids.setdefault(key, len(ids))

    sent = []

    def send(key, src, dst, dev):
        i = sem(key)
        cp = pltpu.make_async_remote_copy(
            src, dst, ss.at[i], rs.at[i], device_id=dev, device_id_type=MESH
        )
        cp.start()
        sent.append(cp)

    def recv(key, ref):
        i = sem(key)
        pltpu.make_async_remote_copy(
            ref, ref, ss.at[i], rs.at[i], device_id=(s, t), device_id_type=MESH
        ).wait_recv()

    def part(bufs, ch, p, half=None):
        g, xx = bufs
        base = p * PIECE
        if ch == X:
            rows = pl.ds(pl.multiple_of(base, PIECE), PIECE)
            return xx.at[:, rows] if half is None else xx.at[half, rows]
        if half is None:
            return g.at[ch // 2, pl.ds(pl.multiple_of(base, PIECE), PIECE)]
        h = PIECE // 2
        return g.at[ch // 2, pl.ds(pl.multiple_of(base + half * h, SUB), h)]

    F, S = (fg, fx), (sg, sx)

    for ch in (GA, X, GB):
        for k in range(1, N):
            p = (s + k) % N
            send(("a", ch, k), share(ch, p), slot(ch, k - 1), (p, t))

    def pick(ch):
        own[ch].wait()
        for k in range(1, N):
            recv(("a", ch, k), slot(ch, k - 1))
        for u in range(USES):
            k = (s - use[u] + 2 * N - 1) % N
            rows = pl.ds(pl.multiple_of(s * PIECE + u * SUB, SUB), SUB)
            if ch == X:
                both = rx[k]
                fx[0, rows, :] = both[:SUB]
                fx[1, rows, :] = both[SUB:]
            else:
                fg[ch // 2, rows, :] = (rg0, rx, rg1)[ch][k]

    def mirror(ch):
        i = sem(("t", ch))
        src, dst = part(F, ch, s), part(S, ch, s)

        @pl.when(s != t)
        def _():
            pltpu.make_async_remote_copy(
                src, dst, ss.at[i], rs.at[i], device_id=(t, s), device_id_type=MESH
            ).start()

        @pl.when(s == t)
        def _():
            pltpu.make_async_copy(src, dst, rs.at[i]).start()

    def mirror_sent(ch):
        i = sem(("t", ch))

        @pl.when(s != t)
        def _():
            ref = part(F, ch, s)
            pltpu.make_async_remote_copy(
                ref, ref, ss.at[i], rs.at[i], device_id=(t, s), device_id_type=MESH
            ).wait_send()

    def along_x(ch, dz):
        p = sec(0, dz)
        for d in (1, -1):
            send(("x", ch, dz, d), part(F, ch, p), part(F, ch, p), (sec(d, 0), t))

    def along_z(ch):
        for d in (1, -1):
            send(("z", ch, d), part(F, ch, s), part(F, ch, s), (sec(0, d), t))

    def z_in(ch):
        for d in (1, -1):
            p = sec(0, -d)
            recv(("z", ch, d), part(F, ch, p))
            r = part(F, ch, p, (1 - d) // 2)
            send(("zf", ch, d), r, r, (sec(0, d), t))
            along_x(ch, -d)

    def z_far(ch):
        for d in (1, -1):
            recv(("zf", ch, d), part(F, ch, sec(0, 2), (1 - d) // 2))
        along_x(ch, 2)

    def x_in(ch, dz):
        for d in (1, -1):
            p = sec(-d, dz)
            recv(("x", ch, dz, d), part(F, ch, p))
            r = part(F, ch, p, (1 - d) // 2)
            send(("xf", ch, dz, d), r, r, (sec(d, 0), t))

    def x_far(ch, dz):
        for d in (1, -1):
            recv(("xf", ch, dz, d), part(F, ch, sec(2, dz), (1 - d) // 2))

    def to_core(ch, dl, dy):
        p = ten(dl, dy, 0)
        send(("c", ch, dl, dy), part(S, ch, p), part(S, ch, p), (s, ten(0, 0, 1)))

    def along_y(ch, dl):
        p = ten(dl, 0, 0)
        for d in (1, -1):
            send(("y", ch, dl, d), part(S, ch, p), part(S, ch, p), (s, ten(0, d, 0)))

    def plane_start(ch):
        recv(("t", ch), part(S, ch, t))
        send(("l", ch), part(S, ch, t), part(S, ch, t), (s, ten(1, 0, 0)))
        along_y(ch, 0)
        to_core(ch, 0, 0)

    def plane_l(ch):
        recv(("l", ch), part(S, ch, ten(1, 0, 0)))
        along_y(ch, 1)
        to_core(ch, 1, 0)

    def plane_y(ch, dl):
        for d in (1, -1):
            p = ten(dl, -d, 0)
            recv(("y", ch, dl, d), part(S, ch, p))
            r = part(S, ch, p, (1 - d) // 2)
            send(("yf", ch, dl, d), r, r, (s, ten(0, d, 0)))
            to_core(ch, dl, -d)

    def plane_far(ch, dl):
        for d in (1, -1):
            recv(("yf", ch, dl, d), part(S, ch, ten(dl, 2, 0), (1 - d) // 2))
        to_core(ch, dl, 2)

    def plane_core(ch):
        for dl in (0, 1):
            for dy in (0, 1, -1, 2):
                recv(("c", ch, dl, dy), part(S, ch, ten(dl, dy, 1)))

    def g_step(h, first):
        step = HALF // 3
        for i in range(3):
            rows = pl.ds(i * step, step)
            prod = cross(sg[h, rows, :], fg[h, rows, :])
            if first and i == 0:
                acc_g[...] = prod
            else:
                acc_g[...] += prod

    def w_step(h):
        prod = cross(sx[h], fg[h])
        if h == 0:
            acc_w[...] = prod
        else:
            acc_w[...] += prod

    pick(GA)
    mirror(GA)
    along_z(GA)
    along_x(GA, 0)
    pick(X)
    mirror(X)
    plane_start(GA)
    z_in(GA)
    pick(GB)
    mirror(GB)
    along_z(GB)
    along_x(GB, 0)
    plane_start(X)
    plane_l(GA)
    x_in(GA, 0)
    z_far(GA)
    plane_y(GA, 0)
    plane_start(GB)
    z_in(GB)
    x_in(GA, -1)
    x_in(GA, 1)
    plane_l(X)
    plane_y(GA, 1)
    plane_far(GA, 0)
    plane_l(GB)
    x_in(GB, 0)
    z_far(GB)
    x_in(GA, 2)
    plane_y(X, 0)
    plane_y(GB, 0)
    plane_far(GA, 1)
    along_z(X)
    along_x(X, 0)
    x_in(GB, -1)
    x_in(GB, 1)
    plane_y(X, 1)
    plane_far(X, 0)
    plane_y(GB, 1)
    plane_far(GB, 0)
    plane_far(X, 1)
    z_in(X)
    x_in(GB, 2)
    plane_far(GB, 1)
    for dz in (0, -1, 1, 2):
        x_far(GA, dz)
    plane_core(GA)
    g_step(0, True)
    x_in(X, 0)
    z_far(X)
    plane_core(X)
    w_step(0)
    x_in(X, -1)
    x_in(X, 1)
    for dz in (0, -1, 1, 2):
        x_far(GB, dz)
    plane_core(GB)
    w_step(1)
    x_in(X, 2)
    outs = [pltpu.make_async_copy(acc_w, w_out, ls.at[5])]
    outs[-1].start()
    g_step(1, False)
    outs.append(pltpu.make_async_copy(acc_g, g_out, ls.at[6]))
    outs[-1].start()
    for cp in loads:
        cp.wait()
    left = jnp.dot(
        ai[...], acc_w[...], precision=lax.Precision.HIGHEST, preferred_element_type=jnp.float32
    )
    acc_p[...] = jnp.dot(
        left, gi[...], precision=lax.Precision.HIGHEST, preferred_element_type=jnp.float32
    )
    outs.append(pltpu.make_async_copy(acc_p, p_out, ls.at[7]))
    outs[-1].start()
    for dz in (0, -1, 1, 2):
        x_far(X, dz)
    acc_a[...] = (cross(sx[0], fx[0]) + cross(sx[1], fx[1])) / (USES * TOK_DEV)
    outs.append(pltpu.make_async_copy(acc_a, a_out, ls.at[8]))
    outs[-1].start()
    for cp in sent:
        cp.wait_send()
    for ch in range(3):
        mirror_sent(ch)
    for cp in outs:
        cp.wait()
    assert len(ids) <= 192, len(ids)


def on_device(inputs, out_grads, use_section, a_inverse, g_inverse):
    bf, f32 = jnp.bfloat16, jnp.float32
    any_space = pl.BlockSpec(memory_space=pl.ANY)
    return pl.pallas_call(
        kernel,
        out_shape=(
            jax.ShapeDtypeStruct((DB, DB), f32),
            jax.ShapeDtypeStruct((FB, FB), f32),
            jax.ShapeDtypeStruct((DB, FB), f32),
            jax.ShapeDtypeStruct((DB, FB), f32),
        ),
        in_specs=[
            any_space,
            any_space,
            pl.BlockSpec(memory_space=pltpu.SMEM),
            any_space,
            any_space,
        ],
        out_specs=(any_space,) * 4,
        scratch_shapes=[
            pltpu.VMEM((N, SUB, FB), bf),
            pltpu.VMEM((N, SUB, FB), bf),
            pltpu.VMEM((N, 2 * SUB, DB), bf),
            pltpu.VMEM((2, HALF, FB), bf),
            pltpu.VMEM((2, HALF, DB), bf),
            pltpu.VMEM((2, HALF, FB), bf),
            pltpu.VMEM((2, HALF, DB), bf),
            pltpu.VMEM((DB, DB), f32),
            pltpu.VMEM((FB, FB), f32),
            pltpu.VMEM((DB, FB), f32),
            pltpu.VMEM((DB, FB), f32),
            pltpu.VMEM((DB, DB), f32),
            pltpu.VMEM((FB, FB), f32),
            pltpu.SemaphoreType.DMA((192,)),
            pltpu.SemaphoreType.DMA((192,)),
            pltpu.SemaphoreType.DMA((9,)),
        ],
        compiler_params=pltpu.CompilerParams(
            collective_id=0, has_side_effects=True, vmem_limit_bytes=48 * 2**20
        ),
        name="kfac",
    )(inputs, out_grads, use_section, a_inverse, g_inverse)


def solution(mesh):
    return jax.shard_map(
        on_device,
        mesh=mesh,
        in_specs=(
            P("section", None),
            P("section", "tensor"),
            P(),
            P("section", None),
            P("tensor", None),
        ),
        out_specs=(
            P("section", "tensor"),
            P("section", "tensor"),
            P("section", "tensor"),
            P("section", "tensor"),
        ),
        check_vma=False,
    )
```

```python
import jax
import jax.numpy as jnp
from jax import lax
from jax.experimental import pallas as pl
from jax.experimental.pallas import tpu as pltpu
from jax.sharding import PartitionSpec as P

TOK_DEV = 512
USES = 6
N = 16
D = 4096
DB = 256
FB = 688
SUB = 16
PIECE = USES * SUB
HALF = N * PIECE
GA, X, GB = 0, 1, 2
DX = (0, 1, -1, 2)
MESH = pl.DeviceIdType.MESH


def cross(left, right):
    return lax.dot_general(
        left, right, (((0,), (0,)), ((), ())), preferred_element_type=jnp.float32
    )


def halves(value):
    high = value.astype(jnp.bfloat16)
    return high, (value - high.astype(jnp.float32)).astype(jnp.bfloat16)


def exact(left, right, i, j):
    def dot(p, q):
        return lax.dot_general(
            p, q, (((i,), (j,)), ((), ())), preferred_element_type=jnp.float32
        )

    (lh, ll), (rh, rl) = halves(left), halves(right)
    return dot(lh, rh) + (dot(lh, rl) + dot(ll, rh))


def aligned(value, step):
    return pl.multiple_of(value * step, step)


def kernel(
    inp, grads, use, a_inv, g_inv, a_out, g_out, w_out, p_out,
    rg0, rg1, rx, mg, mx, fg, fx, sg, sx, acc_a, acc_g, acc_w, acc_p, ai, gi, ss, rs, ls,
):
    s, t = lax.axis_index("section"), lax.axis_index("tensor")
    x, z = s // 4, s % 4
    l, y, c = t // 8, (t // 2) % 4, t % 2

    def sec(dx, dz):
        return ((x + dx + 8) % 4) * 4 + (z + dz + 8) % 4

    def ten(dl, dy, dc):
        return (((l + dl) % 2) * 4 + (y + dy + 4) % 4) * 2 + (c + dc) % 2

    bar = pltpu.get_barrier_semaphore()
    for k in range(1, N):
        pl.semaphore_signal(bar, inc=1, device_id=((s + k) % N, t), device_id_type=MESH)
    for d in (ten(1, 0, 0), ten(0, 1, 0), ten(0, -1, 0), ten(0, 0, 1)):
        pl.semaphore_signal(bar, inc=1, device_id=(s, d), device_id_type=MESH)

    def place(a, b, d):
        return l * 8 + a * 4 + b * 2 + d

    x0, z1, z0 = x % 2, z // 2, z % 2
    swap = place((y // 2 + x0) % 2, (c + z0) % 2, (y % 2 + z1) % 2)
    back = place((y // 2 + x0) % 2, (c + z1) % 2, (y % 2 + z0) % 2)

    @pl.when(swap != t)
    def _():
        pl.semaphore_signal(bar, inc=1, device_id=(s, back), device_id_type=MESH)

    loads = [
        pltpu.make_async_copy(a_inv, ai, ls.at[0]),
        pltpu.make_async_copy(g_inv, gi, ls.at[1]),
    ]

    def share(ch, p):
        if ch == X:
            return inp.at[pl.ds(aligned(p, 2 * SUB), 2 * SUB), pl.ds(aligned(t, DB), DB)]
        h = ch // 2
        return grads.at[pl.ds(pl.multiple_of(p * 2 * SUB + h * SUB, SUB), SUB)]

    def slot(ch, k):
        return (rg0, rx, rg1)[ch].at[k]

    own = [pltpu.make_async_copy(share(ch, s), slot(ch, N - 1), ls.at[2 + ch]) for ch in range(3)]
    for cp in loads + own:
        cp.start()
    pl.semaphore_wait(bar, 19 + (swap != t).astype(jnp.int32))

    ids = {}

    def sem(key):
        return ids.setdefault(key, len(ids))

    sent = []
    late = []

    def send(key, src, dst, dev):
        i = sem(key)
        cp = pltpu.make_async_remote_copy(
            src, dst, ss.at[i], rs.at[i], device_id=dev, device_id_type=MESH
        )
        cp.start()
        sent.append(cp)

    def recv(key, ref):
        recv_at(sem(key), ref)

    def recv_at(i, ref):
        pltpu.make_async_remote_copy(
            ref, ref, ss.at[i], rs.at[i], device_id=(s, t), device_id_type=MESH
        ).wait_recv()

    def part(bufs, ch, p, half=None):
        g, xx = bufs
        base = p * PIECE
        if ch == X:
            rows = pl.ds(pl.multiple_of(base, PIECE), PIECE)
            return xx.at[:, rows] if half is None else xx.at[half, rows]
        if half is None:
            return g.at[ch // 2, pl.ds(pl.multiple_of(base, PIECE), PIECE)]
        h = PIECE // 2
        return g.at[ch // 2, pl.ds(pl.multiple_of(base + half * h, SUB), h)]

    F, S = (fg, fx), (sg, sx)

    def deal(ch):
        for k in range(1, N):
            p = (s + k) % N
            send(("a", ch, k), share(ch, p), slot(ch, k - 1), (p, t))

    def pick(ch):
        own[ch].wait()
        for k in range(1, N):
            recv(("a", ch, k), slot(ch, k - 1))
        for u in range(USES):
            k = (s - use[u] + 2 * N - 1) % N
            rows = pl.ds(pl.multiple_of(s * PIECE + u * SUB, SUB), SUB)
            if ch == X:
                both = rx[k]
                fx[0, rows, :] = both[:SUB]
                fx[1, rows, :] = both[SUB:]
            else:
                fg[ch // 2, rows, :] = (rg0, rx, rg1)[ch][k]

    def along_x(ch, dz):
        p = sec(0, dz)
        for d in (1, -1):
            send(("x", ch, dz, d), part(F, ch, p), part(F, ch, p), (sec(d, 0), t))

    def along_z(ch):
        for d in (1, -1):
            send(("z", ch, d), part(F, ch, s), part(F, ch, s), (sec(0, d), t))

    def z_in(ch):
        i = sem(("zf", ch))
        for d in (1, -1):
            p = sec(0, -d)
            ref = part(F, ch, p)
            recv(("z", ch, d), ref)

            @pl.when(x // 2 == (1 + d) // 2)
            def _():
                pltpu.make_async_remote_copy(
                    ref, ref, ss.at[i], rs.at[i], device_id=(sec(0, d), t), device_id_type=MESH
                ).start()

            along_x(ch, -d)

        def sent_all():
            ref = part(F, ch, s)
            pltpu.make_async_copy(ref, ref, ss.at[i]).wait()

        late.append(sent_all)

    def z_far(ch):
        recv(("zf", ch), part(F, ch, sec(0, 2)))
        along_x(ch, 2)

    def x_in(ch, dz):
        for d in (1, -1):
            p = sec(-d, dz)
            recv(("x", ch, dz, d), part(F, ch, p))
            r = part(F, ch, p, (1 - d) // 2)
            send(("xf", ch, dz, d), r, r, (sec(d, 0), t))

    def x_far(ch, dz):
        for d in (1, -1):
            recv(("xf", ch, dz, d), part(F, ch, sec(2, dz), (1 - d) // 2))

    ring = l == s // 8

    def mid(ch):
        return mx if ch == X else mg.at[ch // 2]

    def guarded(out, i, here, src, dst, dev):
        @pl.when(jnp.logical_not(here))
        def _():
            pltpu.make_async_remote_copy(
                src, dst, ss.at[out], rs.at[i], device_id=dev, device_id_type=MESH
            ).start()

        @pl.when(here)
        def _():
            pltpu.make_async_copy(src, dst, rs.at[i]).start()

        def sent_all():
            @pl.when(jnp.logical_not(here))
            def _():
                pltpu.make_async_copy(src, src, ss.at[out]).wait()

        late.append(sent_all)

    def turn_y(ch):
        i = sem(("t1", ch))
        guarded(i, i, swap == t, part(F, ch, s), mid(ch), (s, swap))

    def turn_s(ch):
        recv(("t1", ch), mid(ch))
        to = back
        i = sem(("t2", ch, 0))
        assert sem(("t2", ch, 1)) == i + 1
        guarded(i, i + s // 8, s == to, mid(ch), part(S, ch, s), (to, t))

    def mine(dy, dc, e):
        yy, cc = (y + dy + 4) % 4, (c + dc) % 2
        return 8 * e + (yy // 2 + x0) % 2 * 4 + (cc + z1) % 2 * 2 + (yy % 2 + z0) % 2

    def push(key, ch, p, dev, half=None):
        ref = part(S, ch, p, half)
        send(key, ref, ref, dev)

    def over_l(ch, e):
        p = mine(0, 0, e)
        ref = part(S, ch, p)
        i = sem(("l", ch, e))

        @pl.when(ring)
        def _():
            recv(("t2", ch, e), ref)
            pltpu.make_async_remote_copy(
                ref, ref, ss.at[i], rs.at[i], device_id=(s, ten(1, 0, 0)), device_id_type=MESH
            ).start()

        def sent_all():
            @pl.when(ring)
            def _():
                pltpu.make_async_copy(ref, ref, ss.at[i]).wait()

        late.append(sent_all)

    def start(ch, e):
        p = mine(0, 0, e)

        @pl.when(jnp.logical_not(ring))
        def _():
            recv(("l", ch, e), part(S, ch, p))

        for d in (1, -1):
            push(("y", ch, e, d), ch, p, (s, ten(0, d, 0)))
        push(("c", ch, e, 0), ch, p, (s, ten(0, 0, 1)))

    def y_in(ch, e):
        for d in (1, -1):
            p = mine(-d, 0, e)
            recv(("y", ch, e, d), part(S, ch, p))
            push(("yf", ch, e, d), ch, p, (s, ten(0, d, 0)), (1 - d) // 2)
            push(("c", ch, e, -d), ch, p, (s, ten(0, 0, 1)))

    def y_far(ch, e):
        p = mine(2, 0, e)
        for d in (1, -1):
            recv(("yf", ch, e, d), part(S, ch, p, (1 - d) // 2))
        push(("c", ch, e, 2), ch, p, (s, ten(0, 0, 1)))

    def c_in(ch):
        for e in (0, 1):
            for dy in DX:
                recv(("c", ch, e, dy), part(S, ch, mine(dy, 1, e)))

    def g_step(h, dx):
        rows = pl.ds(pl.multiple_of(sec(dx, -z) * PIECE, 4 * PIECE), 4 * PIECE)
        prod = cross(sg[h, rows, :], fg[h, rows, :])
        if h == 0 and dx == 0:
            acc_g[...] = prod
        else:
            acc_g[...] += prod

    def w_step(h, dx):
        rows = pl.ds(pl.multiple_of(sec(dx, -z) * PIECE, 4 * PIECE), 4 * PIECE)
        prod = cross(fg[h, rows, :], sx[h, rows, :])
        if h == 0 and dx == 0:
            acc_w[...] = prod
        else:
            acc_w[...] += prod

    deal(GA)
    deal(X)
    deal(GB)
    pick(GA)
    turn_y(GA)
    along_x(GA, 0)
    turn_s(GA)
    along_z(GA)
    pick(X)
    turn_y(X)
    along_x(X, 0)
    turn_s(X)
    pick(GB)
    turn_y(GB)
    along_x(GB, 0)
    turn_s(GB)
    along_z(GB)
    z_in(GA)
    x_in(GA, 0)
    over_l(GA, 0)
    over_l(GA, 1)
    over_l(X, 0)
    over_l(X, 1)
    x_in(GB, 0)
    start(GA, 0)
    start(GA, 1)
    z_in(GB)
    along_z(X)
    z_far(GA)
    over_l(GB, 0)
    over_l(GB, 1)
    start(X, 0)
    start(X, 1)
    x_far(GA, 0)
    x_in(GA, -1)
    x_in(GA, 1)
    y_in(GA, 0)
    y_in(GA, 1)
    z_far(GB)
    start(GB, 0)
    start(GB, 1)
    x_in(GA, 2)
    x_far(GB, 0)
    z_in(X)
    x_far(GA, -1)
    x_far(GA, 1)
    x_in(X, 0)
    y_in(X, 0)
    y_in(X, 1)
    y_far(GA, 0)
    y_far(GA, 1)
    x_in(GB, -1)
    x_in(GB, 1)
    z_far(X)
    y_in(GB, 0)
    y_in(GB, 1)
    y_far(X, 0)
    y_far(X, 1)
    x_in(GB, 2)
    x_far(GA, 2)
    x_in(X, -1)
    x_in(X, 1)
    y_far(GB, 0)
    y_far(GB, 1)
    c_in(GA)
    g_step(0, 0)
    x_far(GB, -1)
    x_far(GB, 1)
    x_in(X, 2)
    g_step(0, 1)
    g_step(0, -1)
    g_step(0, 2)
    c_in(X)
    w_step(0, 0)
    w_step(0, 1)
    w_step(0, -1)
    w_step(0, 2)
    w_step(1, 0)
    w_step(1, 1)
    w_step(1, -1)
    c_in(GB)
    g_step(1, 0)
    g_step(1, 1)
    g_step(1, -1)
    x_far(GB, 2)
    w_step(1, 2)
    outs = [pltpu.make_async_copy(acc_w, w_out, ls.at[5])]
    outs[-1].start()
    g_step(1, 2)
    outs.append(pltpu.make_async_copy(acc_g, g_out, ls.at[6]))
    outs[-1].start()
    for cp in loads:
        cp.wait()
    left = exact(acc_w[...], ai[...], 1, 1)
    acc_p[...] = exact(gi[...], left, 0, 0)
    outs.append(pltpu.make_async_copy(acc_p, p_out, ls.at[7]))
    outs[-1].start()
    for dz in DX:
        x_far(X, dz)
    acc_a[...] = (cross(sx[0], fx[0]) + cross(sx[1], fx[1])) / (USES * TOK_DEV)
    outs.append(pltpu.make_async_copy(acc_a, a_out, ls.at[8]))
    outs[-1].start()
    for cp in sent:
        cp.wait_send()
    for wait in late:
        wait()

    for cp in outs:
        cp.wait()
    assert len(ids) <= 256, len(ids)


def on_device(inputs, out_grads, use_section, a_inverse, g_inverse):
    bf, f32 = jnp.bfloat16, jnp.float32
    hbm = pl.BlockSpec(memory_space=pltpu.HBM)
    a_cov, g_cov, grad, precond = pl.pallas_call(
        kernel,
        out_shape=(
            jax.ShapeDtypeStruct((DB, DB), f32),
            jax.ShapeDtypeStruct((FB, FB), f32),
            jax.ShapeDtypeStruct((FB, DB), f32),
            jax.ShapeDtypeStruct((FB, DB), f32),
        ),
        in_specs=[
            hbm,
            hbm,
            pl.BlockSpec(memory_space=pltpu.SMEM),
            hbm,
            hbm,
        ],
        out_specs=(hbm,) * 4,
        scratch_shapes=[
            pltpu.VMEM((N, SUB, FB), bf),
            pltpu.VMEM((N, SUB, FB), bf),
            pltpu.VMEM((N, 2 * SUB, DB), bf),
            pltpu.VMEM((2, PIECE, FB), bf),
            pltpu.VMEM((2, PIECE, DB), bf),
            pltpu.VMEM((2, HALF, FB), bf),
            pltpu.VMEM((2, HALF, DB), bf),
            pltpu.VMEM((2, HALF, FB), bf),
            pltpu.VMEM((2, HALF, DB), bf),
            pltpu.VMEM((DB, DB), f32),
            pltpu.VMEM((FB, FB), f32),
            pltpu.VMEM((FB, DB), f32),
            pltpu.VMEM((FB, DB), f32),
            pltpu.VMEM((DB, DB), f32),
            pltpu.VMEM((FB, FB), f32),
            pltpu.SemaphoreType.DMA((256,)),
            pltpu.SemaphoreType.DMA((256,)),
            pltpu.SemaphoreType.DMA((9,)),
        ],
        compiler_params=pltpu.CompilerParams(
            collective_id=0, has_side_effects=True, vmem_limit_bytes=48 * 2**20
        ),
        name="kfac",
    )(inputs, out_grads, use_section, a_inverse, g_inverse)
    return a_cov, g_cov, grad.T, precond.T


def solution(mesh):
    return jax.shard_map(
        on_device,
        mesh=mesh,
        in_specs=(
            P("section", None),
            P("section", "tensor"),
            P(),
            P("section", None),
            P("tensor", None),
        ),
        out_specs=(
            P("section", "tensor"),
            P("section", "tensor"),
            P("section", "tensor"),
            P("section", "tensor"),
        ),
        check_vma=False,
    )
```

```python
import jax
import jax.numpy as jnp
from jax import lax
from jax.experimental import pallas as pl
from jax.experimental.pallas import tpu as pltpu
from jax.sharding import PartitionSpec as P

TOK_DEV = 512
USES = 6
N = 16
D = 4096
DB = 256
FB = 688
SUB = 16
PIECE = USES * SUB
HALF = N * PIECE
GA, X, GB = 0, 1, 2
DX = (0, 1, -1, 2)
MESH = pl.DeviceIdType.MESH


def cross(left, right):
    return lax.dot_general(
        left, right, (((0,), (0,)), ((), ())), preferred_element_type=jnp.float32
    )


def halves(value):
    high = value.astype(jnp.bfloat16)
    return high, (value - high.astype(jnp.float32)).astype(jnp.bfloat16)


def exact(left, right, i, j):
    def dot(p, q):
        return lax.dot_general(
            p, q, (((i,), (j,)), ((), ())), preferred_element_type=jnp.float32
        )

    (lh, ll), (rh, rl) = halves(left), halves(right)
    return dot(lh, rh) + (dot(lh, rl) + dot(ll, rh))


def aligned(value, step):
    return pl.multiple_of(value * step, step)


def kernel(
    inp, grads, use, a_inv, g_inv, a_out, g_out, w_out, p_out,
    rg0, rg1, rx, mg, mx, fg, fx, sg, sx, acc_a, acc_g, acc_w, acc_p, ai, gi, ss, rs, ls,
):
    s, t = lax.axis_index("section"), lax.axis_index("tensor")
    x, z = s // 4, s % 4
    l, y, c = t // 8, (t // 2) % 4, t % 2

    def sec(dx, dz):
        return ((x + dx + 8) % 4) * 4 + (z + dz + 8) % 4

    def ten(dl, dy, dc):
        return (((l + dl) % 2) * 4 + (y + dy + 4) % 4) * 2 + (c + dc) % 2

    bar = pltpu.get_barrier_semaphore()
    for k in range(1, N):
        pl.semaphore_signal(bar, inc=1, device_id=((s + k) % N, t), device_id_type=MESH)
    for d in (ten(1, 0, 0), ten(0, 1, 0), ten(0, -1, 0), ten(0, 0, 1)):
        pl.semaphore_signal(bar, inc=1, device_id=(s, d), device_id_type=MESH)

    def place(a, b, d):
        return l * 8 + a * 4 + b * 2 + d

    x0, z1, z0 = x % 2, z // 2, z % 2
    swap = place((y // 2 + x0) % 2, (c + z0) % 2, (y % 2 + z1) % 2)
    back = place((y // 2 + x0) % 2, (c + z1) % 2, (y % 2 + z0) % 2)

    @pl.when(swap != t)
    def _():
        pl.semaphore_signal(bar, inc=1, device_id=(s, back), device_id_type=MESH)

    loads = [
        pltpu.make_async_copy(a_inv, ai, ls.at[0]),
        pltpu.make_async_copy(g_inv, gi, ls.at[1]),
    ]

    def share(ch, p):
        if ch == X:
            return inp.at[pl.ds(aligned(p, 2 * SUB), 2 * SUB), pl.ds(aligned(t, DB), DB)]
        h = ch // 2
        return grads.at[pl.ds(pl.multiple_of(p * 2 * SUB + h * SUB, SUB), SUB)]

    def slot(ch, k):
        return (rg0, rx, rg1)[ch].at[k]

    own = [pltpu.make_async_copy(share(ch, s), slot(ch, N - 1), ls.at[2 + ch]) for ch in range(3)]
    for cp in loads + own:
        cp.start()
    pl.semaphore_wait(bar, 19 + (swap != t).astype(jnp.int32))

    ids = {}

    def sem(key):
        return ids.setdefault(key, len(ids))

    sent = []
    late = []

    def send(key, src, dst, dev):
        i = sem(key)
        cp = pltpu.make_async_remote_copy(
            src, dst, ss.at[i], rs.at[i], device_id=dev, device_id_type=MESH
        )
        cp.start()
        sent.append(cp)

    def recv(key, ref):
        recv_at(sem(key), ref)

    def recv_at(i, ref):
        pltpu.make_async_remote_copy(
            ref, ref, ss.at[i], rs.at[i], device_id=(s, t), device_id_type=MESH
        ).wait_recv()

    def part(bufs, ch, p, half=None):
        g, xx = bufs
        base = p * PIECE
        if ch == X:
            rows = pl.ds(pl.multiple_of(base, PIECE), PIECE)
            return xx.at[:, rows] if half is None else xx.at[half, rows]
        if half is None:
            return g.at[ch // 2, pl.ds(pl.multiple_of(base, PIECE), PIECE)]
        h = PIECE // 2
        return g.at[ch // 2, pl.ds(pl.multiple_of(base + half * h, SUB), h)]

    F, S = (fg, fx), (sg, sx)

    def deal(ch):
        for k in range(1, N):
            p = (s + k) % N
            send(("a", ch, k), share(ch, p), slot(ch, k - 1), (p, t))

    def pick(ch):
        own[ch].wait()
        for k in range(1, N):
            recv(("a", ch, k), slot(ch, k - 1))
        for u in range(USES):
            k = (s - use[u] + 2 * N - 1) % N
            rows = pl.ds(pl.multiple_of(s * PIECE + u * SUB, SUB), SUB)
            if ch == X:
                both = rx[k]
                fx[0, rows, :] = both[:SUB]
                fx[1, rows, :] = both[SUB:]
            else:
                fg[ch // 2, rows, :] = (rg0, rx, rg1)[ch][k]

    def along_x(ch, dz):
        p = sec(0, dz)
        for d in (1, -1):
            send(("x", ch, dz, d), part(F, ch, p), part(F, ch, p), (sec(d, 0), t))

    def along_z(ch):
        for d in (1, -1):
            send(("z", ch, d), part(F, ch, s), part(F, ch, s), (sec(0, d), t))

    def z_in(ch):
        i = sem(("zf", ch))
        for d in (1, -1):
            p = sec(0, -d)
            ref = part(F, ch, p)
            recv(("z", ch, d), ref)

            @pl.when(x // 2 == (1 + d) // 2)
            def _():
                pltpu.make_async_remote_copy(
                    ref, ref, ss.at[i], rs.at[i], device_id=(sec(0, d), t), device_id_type=MESH
                ).start()

            along_x(ch, -d)

        def sent_all():
            ref = part(F, ch, s)
            pltpu.make_async_copy(ref, ref, ss.at[i]).wait()

        late.append(sent_all)

    def z_far(ch):
        recv(("zf", ch), part(F, ch, sec(0, 2)))
        along_x(ch, 2)

    def x_in(ch, dz):
        for d in (1, -1):
            p = sec(-d, dz)
            recv(("x", ch, dz, d), part(F, ch, p))
            r = part(F, ch, p, (1 - d) // 2)
            send(("xf", ch, dz, d), r, r, (sec(d, 0), t))

    def x_far(ch, dz):
        for d in (1, -1):
            recv(("xf", ch, dz, d), part(F, ch, sec(2, dz), (1 - d) // 2))

    ring = l == s // 8

    def mid(ch):
        return mx if ch == X else mg.at[ch // 2]

    def guarded(out, i, here, src, dst, dev):
        @pl.when(jnp.logical_not(here))
        def _():
            pltpu.make_async_remote_copy(
                src, dst, ss.at[out], rs.at[i], device_id=dev, device_id_type=MESH
            ).start()

        @pl.when(here)
        def _():
            pltpu.make_async_copy(src, dst, rs.at[i]).start()

        def sent_all():
            @pl.when(jnp.logical_not(here))
            def _():
                pltpu.make_async_copy(src, src, ss.at[out]).wait()

        late.append(sent_all)

    def turn_y(ch):
        i = sem(("t1", ch))
        guarded(i, i, swap == t, part(F, ch, s), mid(ch), (s, swap))

    def turn_s(ch):
        recv(("t1", ch), mid(ch))
        to = back
        i = sem(("t2", ch, 0))
        assert sem(("t2", ch, 1)) == i + 1
        guarded(i, i + s // 8, s == to, mid(ch), part(S, ch, s), (to, t))

    def mine(dy, dc, e):
        yy, cc = (y + dy + 4) % 4, (c + dc) % 2
        return 8 * e + (yy // 2 + x0) % 2 * 4 + (cc + z1) % 2 * 2 + (yy % 2 + z0) % 2

    def push(key, ch, p, dev, half=None):
        ref = part(S, ch, p, half)
        send(key, ref, ref, dev)

    def over_l(ch, e):
        p = mine(0, 0, e)
        ref = part(S, ch, p)
        i = sem(("l", ch, e))

        @pl.when(ring)
        def _():
            recv(("t2", ch, e), ref)
            pltpu.make_async_remote_copy(
                ref, ref, ss.at[i], rs.at[i], device_id=(s, ten(1, 0, 0)), device_id_type=MESH
            ).start()

        def sent_all():
            @pl.when(ring)
            def _():
                pltpu.make_async_copy(ref, ref, ss.at[i]).wait()

        late.append(sent_all)

    def start(ch, e):
        p = mine(0, 0, e)

        @pl.when(jnp.logical_not(ring))
        def _():
            recv(("l", ch, e), part(S, ch, p))

        for d in (1, -1):
            push(("y", ch, e, d), ch, p, (s, ten(0, d, 0)))
        push(("c", ch, e, 0), ch, p, (s, ten(0, 0, 1)))

    def y_in(ch, e):
        for d in (1, -1):
            p = mine(-d, 0, e)
            recv(("y", ch, e, d), part(S, ch, p))
            push(("yf", ch, e, d), ch, p, (s, ten(0, d, 0)), (1 - d) // 2)
            push(("c", ch, e, -d), ch, p, (s, ten(0, 0, 1)))

    def y_far(ch, e):
        p = mine(2, 0, e)
        for d in (1, -1):
            recv(("yf", ch, e, d), part(S, ch, p, (1 - d) // 2))
        push(("c", ch, e, 2), ch, p, (s, ten(0, 0, 1)))

    def c_in(ch):
        for e in (0, 1):
            for dy in DX:
                recv(("c", ch, e, dy), part(S, ch, mine(dy, 1, e)))

    def g_step(h, dx):
        rows = pl.ds(pl.multiple_of(sec(dx, -z) * PIECE, 4 * PIECE), 4 * PIECE)
        prod = cross(sg[h, rows, :], fg[h, rows, :])
        if dx == 0 and h == 0:
            acc_g[...] = prod
        else:
            acc_g[...] += prod

    def g_half(h):
        step = HALF
        for i in range(1):
            rows = pl.ds(i * step, step)
            prod = cross(sg[h, rows, :], fg[h, rows, :])
            if h == 0 and i == 0:
                acc_g[...] = prod
            else:
                acc_g[...] += prod

    def w_half(h):
        prod = cross(fg[h], sx[h])
        if h == 0:
            acc_w[...] = prod
        else:
            acc_w[...] += prod

    def w_step(h, dx):
        rows = pl.ds(pl.multiple_of(sec(dx, -z) * PIECE, 4 * PIECE), 4 * PIECE)
        prod = cross(fg[h, rows, :], sx[h, rows, :])
        if h == 0 and dx == 0:
            acc_w[...] = prod
        else:
            acc_w[...] += prod

    deal(GA)
    deal(X)
    deal(GB)
    pick(GA)
    turn_y(GA)
    along_x(GA, 0)
    along_z(GA)
    turn_s(GA)
    pick(X)
    turn_y(X)
    along_x(X, 0)
    turn_s(X)
    pick(GB)
    turn_y(GB)
    along_x(GB, 0)
    along_z(GB)
    turn_s(GB)
    z_in(GA)
    x_in(GA, 0)
    over_l(GA, 0)
    over_l(GA, 1)
    over_l(X, 0)
    over_l(X, 1)
    x_in(GB, 0)
    start(GA, 0)
    start(GA, 1)
    z_in(GB)
    along_z(X)
    z_far(GA)
    over_l(GB, 0)
    over_l(GB, 1)
    start(X, 0)
    start(X, 1)
    x_far(GA, 0)
    x_in(GA, -1)
    x_in(GA, 1)
    y_in(GA, 0)
    y_in(GA, 1)
    z_far(GB)
    start(GB, 0)
    start(GB, 1)
    x_in(GA, 2)
    x_far(GB, 0)
    z_in(X)
    x_far(GA, -1)
    x_far(GA, 1)
    x_in(X, 0)
    y_in(X, 0)
    y_in(X, 1)
    y_far(GA, 0)
    y_far(GA, 1)
    x_in(GB, -1)
    x_in(GB, 1)
    z_far(X)
    y_in(GB, 0)
    y_in(GB, 1)
    y_far(X, 0)
    y_far(X, 1)
    x_in(GB, 2)
    x_far(GA, 2)
    c_in(GA)
    g_half(0)
    x_in(X, -1)
    x_in(X, 1)
    c_in(X)
    w_half(0)
    y_far(GB, 0)
    y_far(GB, 1)
    w_step(1, 0)
    x_far(GB, -1)
    w_step(1, 1)
    x_far(GB, 1)
    w_step(1, -1)
    x_in(X, 2)
    x_far(GB, 2)
    w_step(1, 2)
    outs = [pltpu.make_async_copy(acc_w, w_out, ls.at[5])]
    outs[-1].start()
    for cp in loads:
        cp.wait()
    left = exact(acc_w[...], ai[...], 1, 1)
    acc_p[...] = exact(gi[...], left, 0, 0)
    outs.append(pltpu.make_async_copy(acc_p, p_out, ls.at[7]))
    outs[-1].start()
    c_in(GB)
    g_half(1)
    outs.append(pltpu.make_async_copy(acc_g, g_out, ls.at[6]))
    outs[-1].start()
    for dz in DX:
        x_far(X, dz)
    acc_a[...] = (cross(sx[0], fx[0]) + cross(sx[1], fx[1])) / (USES * TOK_DEV)
    outs.append(pltpu.make_async_copy(acc_a, a_out, ls.at[8]))
    outs[-1].start()
    for cp in sent:
        cp.wait_send()
    for wait in late:
        wait()

    for cp in outs:
        cp.wait()
    assert len(ids) <= 256, len(ids)


def store(*refs):
    sources, results, sems = refs[:4], refs[4:8], refs[8]
    copies = [
        pltpu.make_async_copy(a, b, sems.at[i]) for i, (a, b) in enumerate(zip(sources, results))
    ]
    for cp in copies:
        cp.start()
    for cp in copies:
        cp.wait()


def on_device(inputs, out_grads, use_section, a_inverse, g_inverse):
    bf, f32 = jnp.bfloat16, jnp.float32
    hbm = pl.BlockSpec(memory_space=pltpu.HBM)
    a_cov, g_cov, grad, precond = pl.pallas_call(
        kernel,
        out_shape=(
            jax.ShapeDtypeStruct((DB, DB), f32),
            jax.ShapeDtypeStruct((FB, FB), f32),
            jax.ShapeDtypeStruct((FB, DB), f32),
            jax.ShapeDtypeStruct((FB, DB), f32),
        ),
        in_specs=[
            hbm,
            hbm,
            pl.BlockSpec(memory_space=pltpu.SMEM),
            hbm,
            hbm,
        ],
        out_specs=(hbm,) * 4,
        scratch_shapes=[
            pltpu.VMEM((N, SUB, FB), bf),
            pltpu.VMEM((N, SUB, FB), bf),
            pltpu.VMEM((N, 2 * SUB, DB), bf),
            pltpu.VMEM((2, PIECE, FB), bf),
            pltpu.VMEM((2, PIECE, DB), bf),
            pltpu.VMEM((2, HALF, FB), bf),
            pltpu.VMEM((2, HALF, DB), bf),
            pltpu.VMEM((2, HALF, FB), bf),
            pltpu.VMEM((2, HALF, DB), bf),
            pltpu.VMEM((DB, DB), f32),
            pltpu.VMEM((FB, FB), f32),
            pltpu.VMEM((FB, DB), f32),
            pltpu.VMEM((FB, DB), f32),
            pltpu.VMEM((DB, DB), f32),
            pltpu.VMEM((FB, FB), f32),
            pltpu.SemaphoreType.DMA((256,)),
            pltpu.SemaphoreType.DMA((256,)),
            pltpu.SemaphoreType.DMA((9,)),
        ],
        compiler_params=pltpu.CompilerParams(
            collective_id=0, has_side_effects=True, vmem_limit_bytes=48 * 2**20
        ),
        name="kfac",
    )(inputs, out_grads, use_section, a_inverse, g_inverse)
    results = (a_cov, g_cov, grad, precond)
    a_cov, g_cov, grad, precond = pl.pallas_call(
        store,
        out_shape=tuple(jax.ShapeDtypeStruct(v.shape, f32) for v in results),
        in_specs=[pl.BlockSpec(memory_space=pl.ANY)] * 4,
        out_specs=(pl.BlockSpec(memory_space=pl.ANY),) * 4,
        scratch_shapes=[pltpu.SemaphoreType.DMA((4,))],
        compiler_params=pltpu.CompilerParams(vmem_limit_bytes=2**20),
        name="store",
    )(*results)
    return a_cov, g_cov, grad.T, precond.T


def solution(mesh):
    return jax.shard_map(
        on_device,
        mesh=mesh,
        in_specs=(
            P("section", None),
            P("section", "tensor"),
            P(),
            P("section", None),
            P("tensor", None),
        ),
        out_specs=(
            P("section", "tensor"),
            P("section", "tensor"),
            P("section", "tensor"),
            P("section", "tensor"),
        ),
        check_vma=False,
    )
```

```python
import jax
import jax.numpy as jnp
from jax import lax
from jax.experimental import pallas as pl
from jax.experimental.pallas import tpu as pltpu
from jax.sharding import PartitionSpec as P

TOK_DEV = 512
USES = 6
N = 16
D = 4096
DB = 256
FB = 688
SUB = 16
PIECE = USES * SUB
HALF = N * PIECE
GA, X, GB = 0, 1, 2
DX = (0, 1, -1, 2)
MESH = pl.DeviceIdType.MESH


def cross(left, right):
    return lax.dot_general(
        left, right, (((0,), (0,)), ((), ())), preferred_element_type=jnp.float32
    )


def halves(value):
    high = value.astype(jnp.bfloat16)
    return high, (value - high.astype(jnp.float32)).astype(jnp.bfloat16)


def exact(left, right, i, j):
    def dot(p, q):
        return lax.dot_general(
            p, q, (((i,), (j,)), ((), ())), preferred_element_type=jnp.float32
        )

    (lh, ll), (rh, rl) = halves(left), halves(right)
    return dot(lh, rh) + (dot(lh, rl) + dot(ll, rh))


def aligned(value, step):
    return pl.multiple_of(value * step, step)


def kernel(
    inp, grads, use, a_inv, g_inv, a_out, g_out, w_out, p_out,
    rg0, rg1, rx, mg, mx, fg, fx, sg, sx, acc_a, acc_g, acc_w, acc_p, ai, gi, ss, rs, ls,
):
    s, t = lax.axis_index("section"), lax.axis_index("tensor")
    x, z = s // 4, s % 4
    l, y, c = t // 8, (t // 2) % 4, t % 2

    def sec(dx, dz):
        return ((x + dx + 8) % 4) * 4 + (z + dz + 8) % 4

    def ten(dl, dy, dc):
        return (((l + dl) % 2) * 4 + (y + dy + 4) % 4) * 2 + (c + dc) % 2

    bar = pltpu.get_barrier_semaphore()
    for k in range(1, N):
        pl.semaphore_signal(bar, inc=1, device_id=((s + k) % N, t), device_id_type=MESH)
    for d in (ten(1, 0, 0), ten(0, 1, 0), ten(0, -1, 0), ten(0, 0, 1)):
        pl.semaphore_signal(bar, inc=1, device_id=(s, d), device_id_type=MESH)

    def place(a, b, d):
        return l * 8 + a * 4 + b * 2 + d

    x0, z1, z0 = x % 2, z // 2, z % 2
    swap = place((y // 2 + x0) % 2, (c + z0) % 2, (y % 2 + z1) % 2)
    back = place((y // 2 + x0) % 2, (c + z1) % 2, (y % 2 + z0) % 2)

    @pl.when(swap != t)
    def _():
        pl.semaphore_signal(bar, inc=1, device_id=(s, back), device_id_type=MESH)

    loads = [
        pltpu.make_async_copy(a_inv, ai, ls.at[0]),
        pltpu.make_async_copy(g_inv, gi, ls.at[1]),
    ]

    def share(ch, p):
        if ch == X:
            return inp.at[pl.ds(aligned(p, 2 * SUB), 2 * SUB), pl.ds(aligned(t, DB), DB)]
        h = ch // 2
        return grads.at[pl.ds(pl.multiple_of(p * 2 * SUB + h * SUB, SUB), SUB)]

    def slot(ch, k):
        return (rg0, rx, rg1)[ch].at[k]

    own = [pltpu.make_async_copy(share(ch, s), slot(ch, N - 1), ls.at[2 + ch]) for ch in range(3)]
    for cp in loads + own:
        cp.start()
    pl.semaphore_wait(bar, 19 + (swap != t).astype(jnp.int32))

    ids = {}

    def sem(key):
        return ids.setdefault(key, len(ids))

    sent = []
    late = []

    def send(key, src, dst, dev):
        i = sem(key)
        cp = pltpu.make_async_remote_copy(
            src, dst, ss.at[i], rs.at[i], device_id=dev, device_id_type=MESH
        )
        cp.start()
        sent.append(cp)

    def recv(key, ref):
        recv_at(sem(key), ref)

    def recv_at(i, ref):
        pltpu.make_async_remote_copy(
            ref, ref, ss.at[i], rs.at[i], device_id=(s, t), device_id_type=MESH
        ).wait_recv()

    def part(bufs, ch, p, half=None):
        g, xx = bufs
        base = p * PIECE
        if ch == X:
            rows = pl.ds(pl.multiple_of(base, PIECE), PIECE)
            return xx.at[:, rows] if half is None else xx.at[half, rows]
        if half is None:
            return g.at[ch // 2, pl.ds(pl.multiple_of(base, PIECE), PIECE)]
        h = PIECE // 2
        return g.at[ch // 2, pl.ds(pl.multiple_of(base + half * h, SUB), h)]

    F, S = (fg, fx), (sg, sx)

    def deal(ch):
        for k in range(1, N):
            p = (s + k) % N
            send(("a", ch, k), share(ch, p), slot(ch, k - 1), (p, t))

    def pick(ch):
        own[ch].wait()
        for k in range(1, N):
            recv(("a", ch, k), slot(ch, k - 1))
        for u in range(USES):
            k = (s - use[u] + 2 * N - 1) % N
            rows = pl.ds(pl.multiple_of(s * PIECE + u * SUB, SUB), SUB)
            if ch == X:
                both = rx[k]
                fx[0, rows, :] = both[:SUB]
                fx[1, rows, :] = both[SUB:]
            else:
                fg[ch // 2, rows, :] = (rg0, rx, rg1)[ch][k]

    def along_x(ch, dz):
        p = sec(0, dz)
        for d in (1, -1):
            send(("x", ch, dz, d), part(F, ch, p), part(F, ch, p), (sec(d, 0), t))

    def along_z(ch):
        for d in (1, -1):
            send(("z", ch, d), part(F, ch, s), part(F, ch, s), (sec(0, d), t))

    def z_in(ch):
        i = sem(("zf", ch))
        for d in (1, -1):
            p = sec(0, -d)
            ref = part(F, ch, p)
            recv(("z", ch, d), ref)

            @pl.when(x // 2 == (1 + d) // 2)
            def _():
                pltpu.make_async_remote_copy(
                    ref, ref, ss.at[i], rs.at[i], device_id=(sec(0, d), t), device_id_type=MESH
                ).start()

            along_x(ch, -d)

        def sent_all():
            ref = part(F, ch, s)
            pltpu.make_async_copy(ref, ref, ss.at[i]).wait()

        late.append(sent_all)

    def z_far(ch):
        recv(("zf", ch), part(F, ch, sec(0, 2)))
        along_x(ch, 2)

    def x_in(ch, dz):
        for d in (1, -1):
            p = sec(-d, dz)
            recv(("x", ch, dz, d), part(F, ch, p))
            r = part(F, ch, p, (1 - d) // 2)
            send(("xf", ch, dz, d), r, r, (sec(d, 0), t))

    def x_far(ch, dz):
        for d in (1, -1):
            recv(("xf", ch, dz, d), part(F, ch, sec(2, dz), (1 - d) // 2))

    ring = l == s // 8

    def mid(ch):
        return mx if ch == X else mg.at[ch // 2]

    def guarded(out, i, here, src, dst, dev):
        @pl.when(jnp.logical_not(here))
        def _():
            pltpu.make_async_remote_copy(
                src, dst, ss.at[out], rs.at[i], device_id=dev, device_id_type=MESH
            ).start()

        @pl.when(here)
        def _():
            pltpu.make_async_copy(src, dst, rs.at[i]).start()

        def sent_all():
            @pl.when(jnp.logical_not(here))
            def _():
                pltpu.make_async_copy(src, src, ss.at[out]).wait()

        late.append(sent_all)

    def turn_y(ch):
        i = sem(("t1", ch))
        guarded(i, i, swap == t, part(F, ch, s), mid(ch), (s, swap))

    def turn_s(ch):
        recv(("t1", ch), mid(ch))
        to = back
        i = sem(("t2", ch, 0))
        assert sem(("t2", ch, 1)) == i + 1
        guarded(i, i + s // 8, s == to, mid(ch), part(S, ch, s), (to, t))

    def mine(dy, dc, e):
        yy, cc = (y + dy + 4) % 4, (c + dc) % 2
        return 8 * e + (yy // 2 + x0) % 2 * 4 + (cc + z1) % 2 * 2 + (yy % 2 + z0) % 2

    def push(key, ch, p, dev, half=None):
        ref = part(S, ch, p, half)
        send(key, ref, ref, dev)

    def over_l(ch, e):
        p = mine(0, 0, e)
        ref = part(S, ch, p)
        i = sem(("l", ch, e))

        @pl.when(ring)
        def _():
            recv(("t2", ch, e), ref)
            pltpu.make_async_remote_copy(
                ref, ref, ss.at[i], rs.at[i], device_id=(s, ten(1, 0, 0)), device_id_type=MESH
            ).start()

        def sent_all():
            @pl.when(ring)
            def _():
                pltpu.make_async_copy(ref, ref, ss.at[i]).wait()

        late.append(sent_all)

    def start(ch, e):
        p = mine(0, 0, e)

        @pl.when(jnp.logical_not(ring))
        def _():
            recv(("l", ch, e), part(S, ch, p))

        for d in (1, -1):
            push(("y", ch, e, d), ch, p, (s, ten(0, d, 0)))
        push(("c", ch, e, 0), ch, p, (s, ten(0, 0, 1)))

    def y_in(ch, e):
        for d in (1, -1):
            p = mine(-d, 0, e)
            recv(("y", ch, e, d), part(S, ch, p))
            push(("yf", ch, e, d), ch, p, (s, ten(0, d, 0)), (1 - d) // 2)
            push(("c", ch, e, -d), ch, p, (s, ten(0, 0, 1)))

    def y_far(ch, e):
        p = mine(2, 0, e)
        for d in (1, -1):
            recv(("yf", ch, e, d), part(S, ch, p, (1 - d) // 2))
        push(("c", ch, e, 2), ch, p, (s, ten(0, 0, 1)))

    def c_in(ch):
        for e in (0, 1):
            for dy in DX:
                recv(("c", ch, e, dy), part(S, ch, mine(dy, 1, e)))

    def g_step(h, dx):
        rows = pl.ds(pl.multiple_of(sec(dx, -z) * PIECE, 4 * PIECE), 4 * PIECE)
        prod = cross(sg[h, rows, :], fg[h, rows, :])
        if dx == 0 and h == 0:
            acc_g[...] = prod
        else:
            acc_g[...] += prod

    def g_half(h):
        step = HALF
        for i in range(1):
            rows = pl.ds(i * step, step)
            prod = cross(sg[h, rows, :], fg[h, rows, :])
            if h == 0 and i == 0:
                acc_g[...] = prod
            else:
                acc_g[...] += prod

    def w_half(h):
        prod = cross(fg[h], sx[h])
        if h == 0:
            acc_w[...] = prod
        else:
            acc_w[...] += prod

    def w_step(h, dx):
        rows = pl.ds(pl.multiple_of(sec(dx, -z) * PIECE, 4 * PIECE), 4 * PIECE)
        prod = cross(fg[h, rows, :], sx[h, rows, :])
        if h == 0 and dx == 0:
            acc_w[...] = prod
        else:
            acc_w[...] += prod

    deal(GA)
    deal(X)
    deal(GB)
    pick(GA)
    turn_y(GA)
    along_x(GA, 0)
    along_z(GA)
    turn_s(GA)
    pick(X)
    turn_y(X)
    along_x(X, 0)
    turn_s(X)
    pick(GB)
    turn_y(GB)
    along_x(GB, 0)
    along_z(GB)
    turn_s(GB)
    z_in(GA)
    x_in(GA, 0)
    over_l(GA, 0)
    over_l(GA, 1)
    over_l(X, 0)
    over_l(X, 1)
    x_in(GB, 0)
    z_in(GB)
    start(GA, 0)
    start(GA, 1)
    z_far(GA)
    over_l(GB, 0)
    over_l(GB, 1)
    along_z(X)
    start(X, 0)
    start(X, 1)
    x_far(GA, 0)
    x_in(GA, -1)
    x_in(GA, 1)
    y_in(GA, 0)
    y_in(GA, 1)
    z_far(GB)
    start(GB, 0)
    start(GB, 1)
    x_in(GA, 2)
    x_far(GB, 0)
    z_in(X)
    x_far(GA, -1)
    x_far(GA, 1)
    x_in(X, 0)
    y_in(X, 0)
    y_in(X, 1)
    y_far(GA, 0)
    y_far(GA, 1)
    x_in(GB, -1)
    x_in(GB, 1)
    z_far(X)
    y_in(GB, 0)
    y_in(GB, 1)
    y_far(X, 0)
    y_far(X, 1)
    x_in(GB, 2)
    x_far(GA, 2)
    c_in(GA)
    g_half(0)
    x_in(X, -1)
    x_in(X, 1)
    c_in(X)
    w_half(0)
    y_far(GB, 0)
    y_far(GB, 1)
    w_step(1, 0)
    x_far(GB, -1)
    w_step(1, 1)
    x_far(GB, 1)
    w_step(1, -1)
    c_in(GB)
    g_step(1, 0)
    x_in(X, 2)
    g_step(1, 1)
    x_far(GB, 2)
    w_step(1, 2)
    outs = [pltpu.make_async_copy(acc_w, w_out, ls.at[5])]
    outs[-1].start()
    for cp in loads:
        cp.wait()
    left = exact(acc_w[...], ai[...], 1, 1)
    acc_p[...] = exact(gi[...], left, 0, 0)
    outs.append(pltpu.make_async_copy(acc_p, p_out, ls.at[7]))
    outs[-1].start()
    g_step(1, -1)
    g_step(1, 2)
    outs.append(pltpu.make_async_copy(acc_g, g_out, ls.at[6]))
    outs[-1].start()
    for dz in DX:
        x_far(X, dz)
    acc_a[...] = (cross(sx[0], fx[0]) + cross(sx[1], fx[1])) / (USES * TOK_DEV)
    outs.append(pltpu.make_async_copy(acc_a, a_out, ls.at[8]))
    outs[-1].start()
    for cp in sent:
        cp.wait_send()
    for wait in late:
        wait()

    for cp in outs:
        cp.wait()
    assert len(ids) <= 256, len(ids)


def store(*refs):
    sources, results, sems = refs[:4], refs[4:8], refs[8]
    copies = [
        pltpu.make_async_copy(a, b, sems.at[i]) for i, (a, b) in enumerate(zip(sources, results))
    ]
    for cp in copies:
        cp.start()
    for cp in copies:
        cp.wait()


def on_device(inputs, out_grads, use_section, a_inverse, g_inverse):
    bf, f32 = jnp.bfloat16, jnp.float32
    hbm = pl.BlockSpec(memory_space=pltpu.HBM)
    a_cov, g_cov, grad, precond = pl.pallas_call(
        kernel,
        out_shape=(
            jax.ShapeDtypeStruct((DB, DB), f32),
            jax.ShapeDtypeStruct((FB, FB), f32),
            jax.ShapeDtypeStruct((FB, DB), f32),
            jax.ShapeDtypeStruct((FB, DB), f32),
        ),
        in_specs=[
            hbm,
            hbm,
            pl.BlockSpec(memory_space=pltpu.SMEM),
            hbm,
            hbm,
        ],
        out_specs=(hbm,) * 4,
        scratch_shapes=[
            pltpu.VMEM((N, SUB, FB), bf),
            pltpu.VMEM((N, SUB, FB), bf),
            pltpu.VMEM((N, 2 * SUB, DB), bf),
            pltpu.VMEM((2, PIECE, FB), bf),
            pltpu.VMEM((2, PIECE, DB), bf),
            pltpu.VMEM((2, HALF, FB), bf),
            pltpu.VMEM((2, HALF, DB), bf),
            pltpu.VMEM((2, HALF, FB), bf),
            pltpu.VMEM((2, HALF, DB), bf),
            pltpu.VMEM((DB, DB), f32),
            pltpu.VMEM((FB, FB), f32),
            pltpu.VMEM((FB, DB), f32),
            pltpu.VMEM((FB, DB), f32),
            pltpu.VMEM((DB, DB), f32),
            pltpu.VMEM((FB, FB), f32),
            pltpu.SemaphoreType.DMA((256,)),
            pltpu.SemaphoreType.DMA((256,)),
            pltpu.SemaphoreType.DMA((9,)),
        ],
        compiler_params=pltpu.CompilerParams(
            collective_id=0, has_side_effects=True, vmem_limit_bytes=48 * 2**20
        ),
        name="kfac",
    )(inputs, out_grads, use_section, a_inverse, g_inverse)
    results = (a_cov, g_cov, grad, precond)
    a_cov, g_cov, grad, precond = pl.pallas_call(
        store,
        out_shape=tuple(jax.ShapeDtypeStruct(v.shape, f32) for v in results),
        in_specs=[pl.BlockSpec(memory_space=pl.ANY)] * 4,
        out_specs=(pl.BlockSpec(memory_space=pl.ANY),) * 4,
        scratch_shapes=[pltpu.SemaphoreType.DMA((4,))],
        compiler_params=pltpu.CompilerParams(vmem_limit_bytes=2**20),
        name="store",
    )(*results)
    return a_cov, g_cov, grad.T, precond.T


def solution(mesh):
    return jax.shard_map(
        on_device,
        mesh=mesh,
        in_specs=(
            P("section", None),
            P("section", "tensor"),
            P(),
            P("section", None),
            P("tensor", None),
        ),
        out_specs=(
            P("section", "tensor"),
            P("section", "tensor"),
            P("section", "tensor"),
            P("section", "tensor"),
        ),
        check_vma=False,
    )
```

```python
import jax
import jax.numpy as jnp
from jax import lax
from jax.experimental import pallas as pl
from jax.experimental.pallas import tpu as pltpu
from jax.sharding import PartitionSpec as P

TOK_DEV = 512
USES = 6
N = 16
D = 4096
DB = 256
FB = 688
SUB = 16
PIECE = USES * SUB
HALF = N * PIECE
GA, X, GB = 0, 1, 2
DX = (0, 1, -1, 2)
MESH = pl.DeviceIdType.MESH


def cross(left, right):
    return lax.dot_general(
        left, right, (((0,), (0,)), ((), ())), preferred_element_type=jnp.float32
    )


def halves(value):
    high = value.astype(jnp.bfloat16)
    return high, (value - high.astype(jnp.float32)).astype(jnp.bfloat16)


def exact(left, right, i, j):
    def dot(p, q):
        return lax.dot_general(
            p, q, (((i,), (j,)), ((), ())), preferred_element_type=jnp.float32
        )

    (lh, ll), (rh, rl) = halves(left), halves(right)
    return dot(lh, rh) + (dot(lh, rl) + dot(ll, rh))


def aligned(value, step):
    return pl.multiple_of(value * step, step)


def kernel(
    inp, grads, use, a_out, g_out, w_out,
    rg0, rg1, rx, mg, mx, fg, fx, sg, sx, acc_a, acc_g, acc_w, ss, rs, ls,
):
    s, t = lax.axis_index("section"), lax.axis_index("tensor")
    x, z = s // 4, s % 4
    l, y, c = t // 8, (t // 2) % 4, t % 2

    def sec(dx, dz):
        return ((x + dx + 8) % 4) * 4 + (z + dz + 8) % 4

    def ten(dl, dy, dc):
        return (((l + dl) % 2) * 4 + (y + dy + 4) % 4) * 2 + (c + dc) % 2

    bar = pltpu.get_barrier_semaphore()
    for k in range(1, N):
        pl.semaphore_signal(bar, inc=1, device_id=((s + k) % N, t), device_id_type=MESH)
    for d in (ten(1, 0, 0), ten(0, 1, 0), ten(0, -1, 0), ten(0, 0, 1)):
        pl.semaphore_signal(bar, inc=1, device_id=(s, d), device_id_type=MESH)

    def place(a, b, d):
        return l * 8 + a * 4 + b * 2 + d

    x0, z1, z0 = x % 2, z // 2, z % 2
    swap = place((y // 2 + x0) % 2, (c + z0) % 2, (y % 2 + z1) % 2)
    back = place((y // 2 + x0) % 2, (c + z1) % 2, (y % 2 + z0) % 2)

    @pl.when(swap != t)
    def _():
        pl.semaphore_signal(bar, inc=1, device_id=(s, back), device_id_type=MESH)


    def share(ch, p):
        if ch == X:
            return inp.at[pl.ds(aligned(p, 2 * SUB), 2 * SUB), pl.ds(aligned(t, DB), DB)]
        h = ch // 2
        return grads.at[pl.ds(pl.multiple_of(p * 2 * SUB + h * SUB, SUB), SUB)]

    def slot(ch, k):
        return (rg0, rx, rg1)[ch].at[k]

    own = [pltpu.make_async_copy(share(ch, s), slot(ch, N - 1), ls.at[2 + ch]) for ch in range(3)]
    for cp in own:
        cp.start()
    pl.semaphore_wait(bar, 19 + (swap != t).astype(jnp.int32))

    ids = {}

    def sem(key):
        return ids.setdefault(key, len(ids))

    sent = []
    late = []

    def send(key, src, dst, dev):
        i = sem(key)
        cp = pltpu.make_async_remote_copy(
            src, dst, ss.at[i], rs.at[i], device_id=dev, device_id_type=MESH
        )
        cp.start()
        sent.append(cp)

    def recv(key, ref):
        recv_at(sem(key), ref)

    def recv_at(i, ref):
        pltpu.make_async_remote_copy(
            ref, ref, ss.at[i], rs.at[i], device_id=(s, t), device_id_type=MESH
        ).wait_recv()

    def part(bufs, ch, p, half=None):
        g, xx = bufs
        base = p * PIECE
        if ch == X:
            rows = pl.ds(pl.multiple_of(base, PIECE), PIECE)
            return xx.at[:, rows] if half is None else xx.at[half, rows]
        if half is None:
            return g.at[ch // 2, pl.ds(pl.multiple_of(base, PIECE), PIECE)]
        h = PIECE // 2
        return g.at[ch // 2, pl.ds(pl.multiple_of(base + half * h, SUB), h)]

    F, S = (fg, fx), (sg, sx)

    def deal(ch):
        for k in range(1, N):
            p = (s + k) % N
            send(("a", ch, k), share(ch, p), slot(ch, k - 1), (p, t))

    def pick(ch):
        own[ch].wait()
        for k in range(1, N):
            recv(("a", ch, k), slot(ch, k - 1))
        for u in range(USES):
            k = (s - use[u] + 2 * N - 1) % N
            rows = pl.ds(pl.multiple_of(s * PIECE + u * SUB, SUB), SUB)
            if ch == X:
                both = rx[k]
                fx[0, rows, :] = both[:SUB]
                fx[1, rows, :] = both[SUB:]
            else:
                fg[ch // 2, rows, :] = (rg0, rx, rg1)[ch][k]

    def along_x(ch, dz):
        p = sec(0, dz)
        for d in (1, -1):
            send(("x", ch, dz, d), part(F, ch, p), part(F, ch, p), (sec(d, 0), t))

    def along_z(ch):
        for d in (1, -1):
            send(("z", ch, d), part(F, ch, s), part(F, ch, s), (sec(0, d), t))

    def z_in(ch):
        i = sem(("zf", ch))
        for d in (1, -1):
            p = sec(0, -d)
            ref = part(F, ch, p)
            recv(("z", ch, d), ref)

            @pl.when(x // 2 == (1 + d) // 2)
            def _():
                pltpu.make_async_remote_copy(
                    ref, ref, ss.at[i], rs.at[i], device_id=(sec(0, d), t), device_id_type=MESH
                ).start()

            along_x(ch, -d)

        def sent_all():
            ref = part(F, ch, s)
            pltpu.make_async_copy(ref, ref, ss.at[i]).wait()

        late.append(sent_all)

    def z_far(ch):
        recv(("zf", ch), part(F, ch, sec(0, 2)))
        along_x(ch, 2)

    def x_in(ch, dz):
        for d in (1, -1):
            p = sec(-d, dz)
            recv(("x", ch, dz, d), part(F, ch, p))
            r = part(F, ch, p, (1 - d) // 2)
            send(("xf", ch, dz, d), r, r, (sec(d, 0), t))

    def x_far(ch, dz):
        for d in (1, -1):
            recv(("xf", ch, dz, d), part(F, ch, sec(2, dz), (1 - d) // 2))

    ring = l == s // 8

    def mid(ch):
        return mx if ch == X else mg.at[ch // 2]

    def guarded(out, i, here, src, dst, dev):
        @pl.when(jnp.logical_not(here))
        def _():
            pltpu.make_async_remote_copy(
                src, dst, ss.at[out], rs.at[i], device_id=dev, device_id_type=MESH
            ).start()

        @pl.when(here)
        def _():
            pltpu.make_async_copy(src, dst, rs.at[i]).start()

        def sent_all():
            @pl.when(jnp.logical_not(here))
            def _():
                pltpu.make_async_copy(src, src, ss.at[out]).wait()

        late.append(sent_all)

    def turn_y(ch):
        i = sem(("t1", ch))
        guarded(i, i, swap == t, part(F, ch, s), mid(ch), (s, swap))

    def turn_s(ch):
        recv(("t1", ch), mid(ch))
        to = back
        i = sem(("t2", ch, 0))
        assert sem(("t2", ch, 1)) == i + 1
        guarded(i, i + s // 8, s == to, mid(ch), part(S, ch, s), (to, t))

    def mine(dy, dc, e):
        yy, cc = (y + dy + 4) % 4, (c + dc) % 2
        return 8 * e + (yy // 2 + x0) % 2 * 4 + (cc + z1) % 2 * 2 + (yy % 2 + z0) % 2

    def push(key, ch, p, dev, half=None):
        ref = part(S, ch, p, half)
        send(key, ref, ref, dev)

    def over_l(ch, e):
        p = mine(0, 0, e)
        ref = part(S, ch, p)
        i = sem(("l", ch, e))

        @pl.when(ring)
        def _():
            recv(("t2", ch, e), ref)
            pltpu.make_async_remote_copy(
                ref, ref, ss.at[i], rs.at[i], device_id=(s, ten(1, 0, 0)), device_id_type=MESH
            ).start()

        def sent_all():
            @pl.when(ring)
            def _():
                pltpu.make_async_copy(ref, ref, ss.at[i]).wait()

        late.append(sent_all)

    def start(ch, e):
        p = mine(0, 0, e)

        @pl.when(jnp.logical_not(ring))
        def _():
            recv(("l", ch, e), part(S, ch, p))

        for d in (1, -1):
            push(("y", ch, e, d), ch, p, (s, ten(0, d, 0)))
        push(("c", ch, e, 0), ch, p, (s, ten(0, 0, 1)))

    def y_in(ch, e):
        for d in (1, -1):
            p = mine(-d, 0, e)
            recv(("y", ch, e, d), part(S, ch, p))
            push(("yf", ch, e, d), ch, p, (s, ten(0, d, 0)), (1 - d) // 2)
            push(("c", ch, e, -d), ch, p, (s, ten(0, 0, 1)))

    def y_far(ch, e):
        p = mine(2, 0, e)
        for d in (1, -1):
            recv(("yf", ch, e, d), part(S, ch, p, (1 - d) // 2))
        push(("c", ch, e, 2), ch, p, (s, ten(0, 0, 1)))

    def c_in(ch):
        for e in (0, 1):
            for dy in DX:
                recv(("c", ch, e, dy), part(S, ch, mine(dy, 1, e)))

    def g_step(h, dx):
        rows = pl.ds(pl.multiple_of(sec(dx, -z) * PIECE, 4 * PIECE), 4 * PIECE)
        prod = cross(sg[h, rows, :], fg[h, rows, :])
        if dx == 0 and h == 0:
            acc_g[...] = prod
        else:
            acc_g[...] += prod

    def g_half(h):
        step = HALF
        for i in range(1):
            rows = pl.ds(i * step, step)
            prod = cross(sg[h, rows, :], fg[h, rows, :])
            if h == 0 and i == 0:
                acc_g[...] = prod
            else:
                acc_g[...] += prod

    def w_half(h):
        prod = cross(fg[h], sx[h])
        if h == 0:
            acc_w[...] = prod
        else:
            acc_w[...] += prod

    def w_step(h, dx):
        rows = pl.ds(pl.multiple_of(sec(dx, -z) * PIECE, 4 * PIECE), 4 * PIECE)
        prod = cross(fg[h, rows, :], sx[h, rows, :])
        if h == 0 and dx == 0:
            acc_w[...] = prod
        else:
            acc_w[...] += prod

    deal(GA)
    deal(X)
    deal(GB)
    pick(GA)
    turn_y(GA)
    along_x(GA, 0)
    along_z(GA)
    turn_s(GA)
    pick(X)
    turn_y(X)
    along_x(X, 0)
    turn_s(X)
    pick(GB)
    turn_y(GB)
    along_x(GB, 0)
    along_z(GB)
    turn_s(GB)
    z_in(GA)
    x_in(GA, 0)
    over_l(GA, 0)
    over_l(GA, 1)
    over_l(X, 0)
    over_l(X, 1)
    x_in(GB, 0)
    start(GA, 0)
    start(GA, 1)
    z_in(GB)
    along_z(X)
    z_far(GA)
    over_l(GB, 0)
    over_l(GB, 1)
    start(X, 0)
    start(X, 1)
    x_far(GA, 0)
    x_in(GA, -1)
    x_in(GA, 1)
    y_in(GA, 0)
    y_in(GA, 1)
    z_far(GB)
    start(GB, 0)
    start(GB, 1)
    x_in(GA, 2)
    x_far(GB, 0)
    z_in(X)
    x_far(GA, -1)
    x_far(GA, 1)
    x_in(X, 0)
    y_in(X, 0)
    y_in(X, 1)
    y_far(GA, 0)
    y_far(GA, 1)
    x_in(GB, -1)
    x_in(GB, 1)
    z_far(X)
    y_in(GB, 0)
    y_in(GB, 1)
    y_far(X, 0)
    y_far(X, 1)
    x_in(GB, 2)
    x_far(GA, 2)
    c_in(GA)
    g_half(0)
    x_in(X, -1)
    x_in(X, 1)
    c_in(X)
    w_half(0)
    y_far(GB, 0)
    y_far(GB, 1)
    w_step(1, 0)
    x_far(GB, -1)
    w_step(1, 1)
    x_far(GB, 1)
    w_step(1, -1)
    x_in(X, 2)
    x_far(GB, 2)
    w_step(1, 2)
    outs = [pltpu.make_async_copy(acc_w, w_out, ls.at[5])]
    outs[-1].start()
    c_in(GB)
    g_half(1)
    outs.append(pltpu.make_async_copy(acc_g, g_out, ls.at[6]))
    outs[-1].start()
    for dz in DX:
        x_far(X, dz)
    acc_a[...] = (cross(sx[0], fx[0]) + cross(sx[1], fx[1])) / (USES * TOK_DEV)
    outs.append(pltpu.make_async_copy(acc_a, a_out, ls.at[8]))
    outs[-1].start()
    for cp in sent:
        cp.wait_send()
    for wait in late:
        wait()

    for cp in outs:
        cp.wait()
    assert len(ids) <= 256, len(ids)


def store(a_cov, g_cov, grad, a_inv, g_inv, a_out, g_out, w_out, p_out, prod, sems):
    copies = [
        pltpu.make_async_copy(p, q, sems.at[i])
        for i, (p, q) in enumerate(((g_cov, g_out), (grad, w_out), (a_cov, a_out)))
    ]
    for cp in copies:
        cp.start()
    prod[...] = exact(g_inv[...], exact(grad[...], a_inv[...], 1, 1), 0, 0)
    copies.append(pltpu.make_async_copy(prod, p_out, sems.at[3]))
    copies[-1].start()
    for cp in copies:
        cp.wait()


def on_device(inputs, out_grads, use_section, a_inverse, g_inverse):
    bf, f32 = jnp.bfloat16, jnp.float32
    hbm = pl.BlockSpec(memory_space=pltpu.HBM)
    a_cov, g_cov, grad = pl.pallas_call(
        kernel,
        out_shape=(
            jax.ShapeDtypeStruct((DB, DB), f32),
            jax.ShapeDtypeStruct((FB, FB), f32),
            jax.ShapeDtypeStruct((FB, DB), f32),
        ),
        in_specs=[
            hbm,
            hbm,
            pl.BlockSpec(memory_space=pltpu.SMEM),
        ],
        out_specs=(hbm,) * 3,
        scratch_shapes=[
            pltpu.VMEM((N, SUB, FB), bf),
            pltpu.VMEM((N, SUB, FB), bf),
            pltpu.VMEM((N, 2 * SUB, DB), bf),
            pltpu.VMEM((2, PIECE, FB), bf),
            pltpu.VMEM((2, PIECE, DB), bf),
            pltpu.VMEM((2, HALF, FB), bf),
            pltpu.VMEM((2, HALF, DB), bf),
            pltpu.VMEM((2, HALF, FB), bf),
            pltpu.VMEM((2, HALF, DB), bf),
            pltpu.VMEM((DB, DB), f32),
            pltpu.VMEM((FB, FB), f32),
            pltpu.VMEM((FB, DB), f32),
            pltpu.SemaphoreType.DMA((256,)),
            pltpu.SemaphoreType.DMA((256,)),
            pltpu.SemaphoreType.DMA((9,)),
        ],
        compiler_params=pltpu.CompilerParams(
            collective_id=0, has_side_effects=True, vmem_limit_bytes=48 * 2**20
        ),
        name="kfac",
    )(inputs, out_grads, use_section)
    vmem = pl.BlockSpec(memory_space=pltpu.VMEM)
    whole = pl.BlockSpec(memory_space=pl.ANY)
    a_cov, g_cov, grad, precond = pl.pallas_call(
        store,
        out_shape=tuple(
            jax.ShapeDtypeStruct(dims, f32) for dims in ((DB, DB), (FB, FB), (FB, DB), (FB, DB))
        ),
        in_specs=[whole, whole, vmem, vmem, vmem],
        out_specs=(whole,) * 4,
        scratch_shapes=[pltpu.VMEM((FB, DB), f32), pltpu.SemaphoreType.DMA((4,))],
        compiler_params=pltpu.CompilerParams(vmem_limit_bytes=24 * 2**20),
        name="store",
    )(a_cov, g_cov, grad, a_inverse, g_inverse)
    return a_cov, g_cov, grad.T, precond.T


def solution(mesh):
    return jax.shard_map(
        on_device,
        mesh=mesh,
        in_specs=(
            P("section", None),
            P("section", "tensor"),
            P(),
            P("section", None),
            P("tensor", None),
        ),
        out_specs=(
            P("section", "tensor"),
            P("section", "tensor"),
            P("section", "tensor"),
            P("section", "tensor"),
        ),
        check_vma=False,
    )
```
